256 devices in a mesh: replica: 32 (over x, z_hi, core), fsdp: 8 (over y, z_lo).
Axes of the slice: x: 4, y: 4, z: 8 (z_hi: 4, z_lo: 2; z = z_hi * 2 + z_lo), core: 2. Of those that a mesh axis runs over, the one named last changes fastest.
Arguments:
- local_frag: bfloat16 [32, 2048, 8192], P('replica', 'fsdp'), may hold values from -6 to 6
- master: float32 [2048, 8192], P('fsdp', 'replica'), may hold values from -6 to 6
- momentum: float32 [2048, 8192], P('fsdp', 'replica'), may hold values from -3 to 3
- counts: int32 [32], P('replica'), may hold values from 1024 to 3072, as said below
- inputs: bfloat16 [32768, 8192], P(('replica', 'fsdp')), may hold values from -6 to 6
- inner_weight: bfloat16 [32, 512, 8192], P('replica', 'fsdp'), may hold values from -0.0625 to 0.0625
- cotangent: bfloat16 [32768, 512], P(('replica', 'fsdp')), may hold values from -6 to 6
Outputs:
- new_master: float32 [2048, 8192], P('fsdp', 'replica')
- new_momentum: float32 [2048, 8192], P('fsdp', 'replica')
- projected: bfloat16 [32768, 512], P(('replica', 'fsdp'))
- input_grad: bfloat16 [32768, 8192], P(('replica', 'fsdp'))
- weight_grad: bfloat16 [32, 512, 8192], P('replica', 'fsdp')
The draws below stay inside these ranges and needn't reach their ends.
Inputs may be any that keep to these rules, and one draw needn't show every extreme that they name: `counts`: one count a replica; the first replica has the least and the last the most.
All inputs are finite; a program needn't handle non-finite values.
Results may differ from the reference program's by a relative error of at most 0.017.
Values may be sent and summed in bfloat16 or wider, within the bound.
No kernel may reach another device: no remote copies, remote signals or barrier semaphores. Data moves between devices by JAX's collectives and lax.ppermute only.
A program may use at most 128 MiB of HBM per device.

```python
import jax
import jax.numpy as jnp
from jax import lax

D = 8192
KVC = 2048
KVI = 512
TOK_DEV = 128
REPLICAS = 32
TOKENS = 32768
N_FSDP = 8


def draw_counts(key, part):
    key = jax.random.fold_in(key, 11)
    index = jnp.arange(REPLICAS, dtype=jnp.int32)
    spread = jax.random.randint(key, (REPLICAS,), 1024, 3073, dtype=jnp.int32)
    first = index == 0
    last = index == REPLICAS - 1
    return jnp.where(first, 1024, jnp.where(last, 3072, spread)).astype(jnp.int32)


def raised(result, key, source, target, parts, factor):
    owner, partner = [(jnp.arange(result.shape[position]) // (result.shape[position] // parts)).reshape([-1 if axis == position else 1 for axis in range(result.ndim)]) for position in (source, target)]
    chosen = jax.random.permutation(key, parts)[partner]
    strong = (owner == chosen) | (owner == (partner + parts // 2) % parts)
    return jnp.where(strong, factor * result, result)


def steps_of(key, dims, pieces, low, high):
    loudness = 1.0
    for axis_at, parts in pieces:
        heights = jax.random.uniform(jax.random.fold_in(jax.random.fold_in(key, 6), axis_at), (parts,), jnp.float32, low / len(pieces), high / len(pieces))
        loudness = loudness * jnp.repeat(jnp.exp(heights), dims[axis_at] // parts).reshape((-1,) + (1,) * (len(dims) - 1 - axis_at))
    return loudness


def noise(stream_key, extent, scale, bound, split=(), kind=jnp.bfloat16):
    array = jax.random.normal(stream_key, extent, jnp.float32) * scale
    if len(split) > 0:
        array = steps_of(stream_key, extent, split, -0.22, 0.18) * array
    return jnp.clip(array, min=-bound, max=bound).astype(kind)


def bell_draw_with(own_key, dims, scale, limit, split, heavy, held_as=jnp.bfloat16):
    values = scale * jax.random.normal(own_key, dims, jnp.float32)
    if split:
        values = values * steps_of(own_key, dims, split, -0.22, 0.18)
    return jnp.clip(raised(values, jax.random.fold_in(own_key, 3), *heavy), -limit, limit).astype(held_as)


def setup_inputs(seed: int = 0) -> dict:
    splits = jax.random.split(jax.random.key(seed), 8)
    return {
        "local_frag": bell_draw_with(splits[0], (REPLICAS, KVC, D), 1.0, 6.0, ((0, 32), (1, 8)), (0, 2, 32, 2.75)),
        "master": noise(splits[1], (KVC, D), 1.0, 6.0, ((0, 8), (1, 32)), jnp.float32),
        "momentum": noise(splits[2], (KVC, D), 0.5, 3.0, ((0, 8), (1, 32)), jnp.float32),
        "counts": draw_counts(jax.random.fold_in(splits[7], 71), 0),
        "inputs": noise(splits[4], (TOKENS, D), 1.0, 6.0, ((0, 256),)),
        "inner_weight": noise(splits[5], (REPLICAS, KVI, D), D ** -0.5, 0.0625, ((0, 32), (1, 8))),
        "cotangent": noise(splits[6], (TOKENS, KVI), 1.0, 6.0, ((0, 256),)),
    }


momentum_decay = 0.9
outer_rate = 0.7


def reference(local_frag, master, momentum, counts, inputs, inner_weight, cotangent):
    weights = counts.astype(jnp.float32)
    count_sum = jnp.sum(weights)

    def accumulate(running, entries):
        return running + entries[0] * entries[1].astype(jnp.float32), None

    summed, _ = lax.scan(accumulate, jnp.zeros((KVC, D), jnp.float32), (weights, local_frag))
    average = summed / count_sum
    pseudo_grad = master - average
    new_momentum = momentum_decay * momentum + pseudo_grad
    new_master = master - outer_rate * (pseudo_grad + momentum_decay * new_momentum)

    grad_scale = 1.0 / (TOK_DEV * N_FSDP)

    def replica_pass(entries):
        tokens_rep, cot_rep, weight_rep = entries
        keys_rep = jnp.dot(tokens_rep, weight_rep.T, preferred_element_type=jnp.float32).astype(jnp.bfloat16)
        back_rep = jnp.dot(cot_rep, weight_rep, preferred_element_type=jnp.float32).astype(jnp.bfloat16)

        def add_device(running, pair):
            tok_block, cot_block = pair
            partial_term = (jnp.dot(cot_block.T, tok_block, preferred_element_type=jnp.float32) * grad_scale).astype(jnp.bfloat16)
            partial_term = lax.optimization_barrier(partial_term)
            return running + partial_term.astype(jnp.float32), None

        grads, _ = lax.scan(add_device, jnp.zeros((KVI, D), jnp.float32),
                            (tokens_rep.reshape(N_FSDP, TOK_DEV, D), cot_rep.reshape(N_FSDP, TOK_DEV, KVI)))
        return keys_rep, back_rep, grads.astype(jnp.bfloat16)

    keys_all, back_all, grad_all = lax.map(
        replica_pass,
        (inputs.reshape(REPLICAS, N_FSDP * TOK_DEV, D), cotangent.reshape(REPLICAS, N_FSDP * TOK_DEV, KVI), inner_weight))
    projected = keys_all.reshape(TOKENS, KVI)
    input_grad = back_all.reshape(TOKENS, D)
    return new_master, new_momentum, projected, input_grad, grad_all
```

```python
import functools

import jax
import jax.numpy as jnp
from jax import lax
from jax.experimental import pallas as pl
from jax.experimental.pallas import tpu as pltpu
from jax.sharding import PartitionSpec as P

momentum_decay = 0.9
outer_rate = 0.7

F32, BF16 = jnp.float32, jnp.bfloat16
ANY = pl.BlockSpec(memory_space=pl.ANY)
VMEM = pl.BlockSpec(memory_space=pltpu.VMEM)
SMEM = pl.BlockSpec(memory_space=pltpu.SMEM)

SEG = 2048
ROWS = 64
TOK = 128
KVI = 512


def y_shift(k):
    return [(f, (f + 2 * k) % 8) for f in range(8)]


Z_SWAP = [(f, f ^ 1) for f in range(8)]
CORE_SWAP = [(r, r ^ 1) for r in range(32)]


def x_shift(k):
    return [(r, (r + 8 * k) % 32) for r in range(32)]


def zh_shift(k):
    return [(r, r // 8 * 8 + (r + 2 * k) % 8) for r in range(32)]


def call(kernel, name, ins, outs, scratch=(), limit=24, flops=0):
    arrays = [a for _, a in ins]
    moved = sum(a.size * a.dtype.itemsize for a in arrays) + sum(
        int(jnp.dtype(o.dtype).itemsize) * o.size for _, o in outs
    )
    return pl.pallas_call(
        kernel,
        name=name,
        in_specs=[s for s, _ in ins],
        out_specs=[s for s, _ in outs],
        out_shape=[o for _, o in outs],
        scratch_shapes=list(scratch),
        compiler_params=pltpu.CompilerParams(vmem_limit_bytes=limit << 20),
        cost_estimate=pl.CostEstimate(flops=flops, bytes_accessed=moved, transcendentals=0),
    )(*arrays)


def shape(*dims, dtype=BF16):
    return jax.ShapeDtypeStruct(dims, dtype)


def here():
    f = lax.axis_index("fsdp")
    return f // 2, f % 2


def run_all(copies):
    for c in copies:
        c.start()
    for c in copies:
        c.wait()


def pack_weight(w, cot, *rest):
    outs, sems = rest[:4], rest[4]
    y, _ = here()
    copies = []
    for k in range(4):
        start = pl.multiple_of((y + k) % 4 * SEG, SEG)
        copies.append((w.at[:, pl.ds(start, SEG)], outs[k].at[pl.ds(0, ROWS)]))
        for j in range(4):
            copies.append((cot.at[pl.ds(32 * j, 32)], outs[k].at[pl.ds(ROWS, 32), pl.ds(KVI * j, KVI)]))
    run_all([pltpu.make_async_copy(s, d, sems.at[i]) for i, (s, d) in enumerate(copies)])


def pack_inputs(x, *rest):
    outs, sems = rest[:4], rest[4]
    y, _ = here()
    copies = []
    for k in range(4):
        start = pl.multiple_of((y + k) % 4 * SEG, SEG)
        copies.append(pltpu.make_async_copy(x.at[:, pl.ds(start, SEG)], outs[k], sems.at[k]))
    run_all(copies)


def unpack_columns(*refs):
    parts, out, sems = refs[:4], refs[4], refs[5]
    y, _ = here()
    copies = []
    for k in range(4):
        start = pl.multiple_of((y + k) % 4 * SEG, SEG)
        copies.append(pltpu.make_async_copy(parts[k], out.at[:, pl.ds(start, SEG)], sems.at[k]))
    run_all(copies)


def grad_to_inputs(*refs):
    got, other, outs, w, cots = refs[:4], refs[4:8], refs[8:12], refs[12], refs[13]
    y, z = here()
    for k in range(4):
        owner = (y + 4 - k) % 4
        w[pl.ds(pl.multiple_of((owner * 2 + z) * ROWS, ROWS), ROWS), :] = got[k][0:ROWS, :]
        w[pl.ds(pl.multiple_of((owner * 2 + 1 - z) * ROWS, ROWS), ROWS), :] = other[k][...]
        for j in range(4):
            cots[TOK * k + 32 * j : TOK * k + 32 * j + 32, :] = got[k][ROWS : ROWS + 32, KVI * j : KVI * j + KVI]
    for c in range(0, SEG, 512):
        part = jnp.dot(cots[...], w[:, c : c + 512], preferred_element_type=F32).astype(BF16)
        for k in range(4):
            outs[k][:, c : c + 512] = part[TOK * k : TOK * k + TOK]


def weight_grad(scale, *refs):
    xs, cots, mine, other, whole = refs[:4], refs[4], refs[5], refs[6], refs[7]
    y, z = here()
    for c in range(0, SEG, 256):
        total = None
        for k in range(4):
            term = lax.dot_general(
                cots[TOK * k : TOK * k + TOK, :],
                xs[k][:, c : c + 256],
                (((0,), (0,)), ((), ())),
                preferred_element_type=F32,
            )
            total = term if total is None else total + term
        whole[:, c : c + 256] = (total * scale).astype(BF16)
    for j in range(4):
        to = (y + j) % 4 * 2
        rows = slice(ROWS * j, ROWS * j + ROWS)
        mine[rows, :] = whole[pl.ds(pl.multiple_of((to + z) * ROWS, ROWS), ROWS), :]
        other[rows, :] = whole[pl.ds(pl.multiple_of((to + 1 - z) * ROWS, ROWS), ROWS), :]


def project(*refs):
    xs, w, outs = refs[:4], refs[4], refs[5:9]
    for k in range(4):
        outs[k][...] = lax.dot_general(
            xs[k][...], w[...], (((1,), (1,)), ((), ())), preferred_element_type=F32
        ).astype(BF16)


def join_grads(mine, recv, *refs):
    parts, outs = refs[:4], refs[4:8]
    for j in range(4):
        rows = slice(ROWS * j, ROWS * j + ROWS)
        outs[j][0:ROWS, :] = (mine[rows, :].astype(F32) + recv[rows, :].astype(F32)).astype(BF16)
        for i in range(4):
            outs[j][ROWS : ROWS + 32, KVI * i : KVI * i + KVI] = parts[(4 - j) % 4][32 * i : 32 * i + 32, :]


def finish(*refs):
    got, grads, keys = refs[:4], refs[4], refs[5]
    y, _ = here()
    for j in range(4):
        owner = (y + 4 - j) % 4
        grads[:, pl.ds(pl.multiple_of(owner * SEG, SEG), SEG)] = got[j][0:ROWS, :]
    for i in range(4):
        total = None
        for j in range(4):
            term = got[j][ROWS : ROWS + 32, KVI * i : KVI * i + KVI].astype(F32)
            total = term if total is None else total + term
        keys[32 * i : 32 * i + 32, :] = total.astype(BF16)


def weigh(counts, mine, other, *outs):
    r = lax.axis_index("replica")
    x, core = r // 8, r % 2
    own, theirs = counts[0], counts[1]
    for k in range(4):
        for h in range(4):
            start = pl.multiple_of((x + k) % 4 * 2048 + h * 512 + core * 256, 256)
            cols = pl.ds(start, 256)
            total = own * mine[:, cols].astype(F32) + theirs * other[:, cols].astype(F32)
            outs[k][:, 256 * h : 256 * h + 256] = total.astype(BF16)


def weigh_grid(frag, frag_other, counts):
    step = 64
    spec_in = pl.BlockSpec((step, 8192), lambda i: (i, 0))
    spec_out = pl.BlockSpec((step, 1024), lambda i: (i, 0))
    return pl.pallas_call(
        weigh,
        name="weigh",
        grid=(256 // step,),
        in_specs=[SMEM, spec_in, spec_in],
        out_specs=[spec_out] * 4,
        out_shape=[shape(256, 1024)] * 4,
        compiler_params=pltpu.CompilerParams(vmem_limit_bytes=24 << 20),
        cost_estimate=pl.CostEstimate(flops=0, bytes_accessed=10 << 20, transcendentals=0),
    )(counts, frag, frag_other)


def sum_blocks(*refs):
    parts, outs = refs[:4], refs[4:8]
    zh = lax.axis_index("replica") // 2 % 4
    for j in range(4):
        cols = pl.ds(pl.multiple_of((zh + j) % 4 * 256, 256), 256)
        total = parts[0][:, cols].astype(F32)
        for p in parts[1:]:
            total = total + p[:, cols].astype(F32)
        outs[j][...] = total.astype(BF16)


def after(value, *others):
    return lax.optimization_barrier((value, *others))[0]


def local(local_frag, master, momentum, counts, inputs, inner_weight, cotangent):
    frag = local_frag[0]
    count = counts.astype(F32)
    frag_other = lax.ppermute(frag, "replica", CORE_SWAP)
    count_other = lax.ppermute(count, "replica", CORE_SWAP)

    dma = pltpu.SemaphoreType.DMA
    sent = call(
        pack_weight,
        "pack_weight",
        [(ANY, inner_weight[0]), (ANY, cotangent)],
        [(ANY, shape(ROWS + 32, SEG))] * 4,
        [dma((20,))],
    )
    got = [sent[0]] + [lax.ppermute(sent[k], "fsdp", y_shift(k)) for k in (1, 2, 3)]
    packed = call(pack_inputs, "pack_inputs", [(ANY, inputs)], [(ANY, shape(TOK, SEG))] * 4, [dma((4,))])
    packed = lax.optimization_barrier((*packed, *got))[:4]
    xs = [packed[0]] + [lax.ppermute(packed[k], "fsdp", y_shift(k)) for k in (1, 2, 3)]
    crossed = [lax.ppermute(g[:ROWS], "fsdp", Z_SWAP) for g in got]

    weights = jnp.concatenate([count, count_other])
    parts = weigh_grid(frag, frag_other, weights)
    pair = count + count_other
    parts = [parts[0]] + [lax.ppermute(parts[k], "replica", x_shift(k)) for k in (1, 2, 3)]
    quad = pair + sum(lax.ppermute(pair, "replica", x_shift(k)) for k in (1, 2, 3))

    flops = 2 * TOK * KVI * 8192
    *back, w_full, cots = call(
        grad_to_inputs,
        "input_grad",
        [(VMEM, a) for a in (*got, *crossed)],
        [(VMEM, shape(TOK, SEG))] * 4 + [(VMEM, shape(KVI, SEG)), (VMEM, shape(4 * TOK, KVI))],
        flops=flops,
    )
    back = [back[0]] + [lax.ppermute(back[k], "fsdp", y_shift(-k)) for k in (1, 2, 3)]

    mine, other = call(
        functools.partial(weight_grad, 1.0 / (TOK * lax.axis_size("fsdp"))),
        "weight_grad",
        [(VMEM, a) for a in (*xs, cots)],
        [(VMEM, shape(4 * ROWS, SEG))] * 2,
        [pltpu.VMEM((KVI, SEG), BF16)],
        flops=flops,
    )
    recv = lax.ppermute(other, "fsdp", Z_SWAP)
    keys = call(
        project,
        "project",
        [(VMEM, a) for a in (*xs, w_full)],
        [(VMEM, shape(TOK, KVI))] * 4,
        flops=flops,
    )

    blocks = call(sum_blocks, "sum_blocks", [(VMEM, a) for a in parts], [(VMEM, shape(256, 256))] * 4)
    blocks = lax.optimization_barrier((*blocks, recv))
    recv = blocks[4]
    shares = [blocks[0]] + [lax.ppermute(blocks[j], "replica", zh_shift(j)) for j in (1, 2, 3)]
    count_sum = quad + sum(lax.ppermute(quad, "replica", zh_shift(j)) for j in (1, 2, 3))

    joined = call(
        join_grads,
        "join_grads",
        [(VMEM, a) for a in (mine, recv, *keys)],
        [(VMEM, shape(ROWS + 32, SEG))] * 4,
    )
    joined = [joined[0]] + [lax.ppermute(joined[j], "fsdp", y_shift(j)) for j in (1, 2, 3)]

    (back_full,) = call(
        unpack_columns, "unpack_input_grad", [(ANY, a) for a in back], [(ANY, shape(TOK, 8192))], [dma((4,))]
    )

    total = shares[0].astype(F32)
    for s in shares[1:]:
        total = total + s.astype(F32)
    pseudo_grad = master - total / count_sum[0]
    new_momentum = momentum_decay * momentum + pseudo_grad
    new_master = master - outer_rate * (pseudo_grad + momentum_decay * new_momentum)

    grads, projected = call(
        finish, "finish", [(VMEM, a) for a in joined], [(VMEM, shape(ROWS, 8192)), (VMEM, shape(TOK, KVI))]
    )
    return new_master, new_momentum, projected, back_full, grads[None]


def solution(mesh):
    placed = (
        P("replica", "fsdp", None),
        P("fsdp", "replica"),
        P("fsdp", "replica"),
        P("replica"),
        P(("replica", "fsdp"), None),
        P("replica", "fsdp", None),
        P(("replica", "fsdp"), None),
    )
    return jax.shard_map(
        local,
        mesh=mesh,
        in_specs=placed,
        out_specs=(
            P("fsdp", "replica"),
            P("fsdp", "replica"),
            P(("replica", "fsdp"), None),
            P(("replica", "fsdp"), None),
            P("replica", "fsdp", None),
        ),
        check_vma=False,
    )
```

```python
import functools

import jax
import jax.numpy as jnp
from jax import lax
from jax.experimental import pallas as pl
from jax.experimental.pallas import tpu as pltpu
from jax.sharding import PartitionSpec as P

momentum_decay = 0.9
outer_rate = 0.7

F32, BF16 = jnp.float32, jnp.bfloat16
ANY = pl.BlockSpec(memory_space=pl.ANY)
VMEM = pl.BlockSpec(memory_space=pltpu.VMEM)
SMEM = pl.BlockSpec(memory_space=pltpu.SMEM)
HBM = pl.BlockSpec(memory_space=pltpu.HBM)

SEG = 2048
ROWS = 64
TOK = 128
KVI = 512


def y_shift(k):
    return [(f, (f + 2 * k) % 8) for f in range(8)]


Z_SWAP = [(f, f ^ 1) for f in range(8)]
CORE_SWAP = [(r, r ^ 1) for r in range(32)]


def x_shift(k):
    return [(r, (r + 8 * k) % 32) for r in range(32)]


ZH_NEAR = [(r, r ^ 2) for r in range(32)]
ZH_FAR = [(r, r ^ 6) for r in range(32)]


def call(kernel, name, ins, outs, scratch=(), limit=24):
    arrays = [a for _, a in ins]
    return pl.pallas_call(
        kernel,
        name=name,
        in_specs=[s for s, _ in ins],
        out_specs=[s for s, _ in outs],
        out_shape=[o for _, o in outs],
        scratch_shapes=list(scratch),
        compiler_params=pltpu.CompilerParams(vmem_limit_bytes=limit << 20),
        cost_estimate=pl.CostEstimate(flops=0, bytes_accessed=0, transcendentals=0),
    )(*arrays)


def shape(*dims, dtype=BF16):
    return jax.ShapeDtypeStruct(dims, dtype)


def here():
    f = lax.axis_index("fsdp")
    return f // 2, f % 2


def run_all(copies):
    for c in copies:
        c.start()
    for c in copies:
        c.wait()


def pack_weight(w, *rest):
    outs, sems = rest[:4], rest[4]
    y, _ = here()
    copies = []
    for k in (1, 3, 2, 0):
        start = pl.multiple_of((y + k) % 4 * SEG, SEG)
        copies.append(pltpu.make_async_copy(w.at[:, pl.ds(start, SEG)], outs[k], sems.at[k]))
    run_all(copies)


def pack_inputs(x, cot, *rest):
    outs, sems = rest[:4], rest[4]
    y, _ = here()
    copies = []
    for k in range(4):
        start = pl.multiple_of((y + k) % 4 * SEG, SEG)
        copies.append((x.at[:, pl.ds(start, SEG)], outs[k].at[pl.ds(0, TOK)]))
        for j in range(4):
            copies.append((cot.at[pl.ds(32 * j, 32)], outs[k].at[pl.ds(TOK, 32), pl.ds(KVI * j, KVI)]))
    run_all([pltpu.make_async_copy(s, d, sems.at[i]) for i, (s, d) in enumerate(copies)])


def unpack_columns(*refs):
    parts, out, sems = refs[:4], refs[4], refs[5]
    y, _ = here()
    copies = []
    for k in range(4):
        start = pl.multiple_of((y + k) % 4 * SEG, SEG)
        copies.append(pltpu.make_async_copy(parts[k], out.at[:, pl.ds(start, SEG)], sems.at[k]))
    run_all(copies)


def stack(*refs):
    for k in range(4):
        refs[4][ROWS * k : ROWS * k + ROWS, :] = refs[k][...]


def grad_to_inputs(*refs):
    got, other, xs, outs, w, cots = refs[:4], refs[4], refs[5:9], refs[9:13], refs[13], refs[14]
    y, z = here()
    for k in range(4):
        owner = (y + 4 - k) % 4
        w[pl.ds(pl.multiple_of((owner * 2 + z) * ROWS, ROWS), ROWS), :] = got[k][...]
        w[pl.ds(pl.multiple_of((owner * 2 + 1 - z) * ROWS, ROWS), ROWS), :] = other[ROWS * k : ROWS * k + ROWS, :]
        for j in range(4):
            cots[TOK * k + 32 * j : TOK * k + 32 * j + 32, :] = xs[k][TOK : TOK + 32, KVI * j : KVI * j + KVI]
    for c in range(0, SEG, 512):
        part = jnp.dot(cots[...], w[:, c : c + 512], preferred_element_type=F32).astype(BF16)
        for k in range(4):
            outs[k][:, c : c + 512] = part[TOK * k : TOK * k + TOK]


def weight_grad(scale, *refs):
    xs, cots, mine, other, whole = refs[:4], refs[4], refs[5], refs[6], refs[7]
    y, z = here()
    for c in range(0, SEG, 256):
        total = None
        for k in range(4):
            term = lax.dot_general(
                cots[TOK * k : TOK * k + TOK, :],
                xs[k][0:TOK, c : c + 256],
                (((0,), (0,)), ((), ())),
                preferred_element_type=F32,
            )
            total = term if total is None else total + term
        whole[:, c : c + 256] = (total * scale).astype(BF16)
    for j in range(4):
        to = (y + j) % 4 * 2
        rows = slice(ROWS * j, ROWS * j + ROWS)
        mine[rows, :] = whole[pl.ds(pl.multiple_of((to + z) * ROWS, ROWS), ROWS), :]
        other[rows, :] = whole[pl.ds(pl.multiple_of((to + 1 - z) * ROWS, ROWS), ROWS), :]


def project(*refs):
    xs, w, outs = refs[:4], refs[4], refs[5:9]
    for k in range(4):
        outs[k][...] = lax.dot_general(
            xs[k][0:TOK, :], w[...], (((1,), (1,)), ((), ())), preferred_element_type=F32
        ).astype(BF16)


def sum_keys(*refs):
    total = refs[0][...].astype(F32)
    for r in refs[1:4]:
        total = total + r[...].astype(F32)
    refs[4][...] = total.astype(BF16)


def join_grads(mine, recv, *outs):
    for j in range(4):
        rows = slice(ROWS * j, ROWS * j + ROWS)
        outs[j][...] = (mine[rows, :].astype(F32) + recv[rows, :].astype(F32)).astype(BF16)


def finish(*refs):
    got, grads = refs[:4], refs[4]
    y, _ = here()
    for j in range(4):
        owner = (y + 4 - j) % 4
        grads[:, pl.ds(pl.multiple_of(owner * SEG, SEG), SEG)] = got[j][...]


def put_count(ref, row, value):
    half = ref.shape[1] // 2
    high = jnp.floor(value * (1.0 / 256.0))
    for i in range(0, half, 128):
        ref[row : row + 16, i : i + 128] = jnp.broadcast_to(high, (16, 128)).astype(BF16)
        ref[row : row + 16, half + i : half + i + 128] = jnp.broadcast_to(value - 256.0 * high, (16, 128)).astype(BF16)


def take_count(refs, row):
    half = refs[0].shape[1] // 2
    total = None
    for r in refs:
        high, low = r[row : row + 16, 0:128].astype(F32), r[row : row + 16, half : half + 128].astype(F32)
        term = high * 256.0 + low
        total = term if total is None else total + term
    return total[0:1, :]


def weigh(counts, counts_other, mine, other, *outs):
    r = lax.axis_index("replica")
    x, core = r // 8, r % 2
    own, theirs = counts[0], counts_other[0]
    for k in range(4):
        for h in range(4):
            start = pl.multiple_of((x + k) % 4 * 2048 + h * 512 + core * 256, 256)
            cols = pl.ds(start, 256)
            total = own * mine[:, cols].astype(F32) + theirs * other[:, cols].astype(F32)
            outs[k][0:256, 256 * h : 256 * h + 256] = total.astype(BF16)
        put_count(outs[k], 256, jnp.full((1, 128), own + theirs, F32))


def sum_blocks(*refs):
    parts, keep, send = refs[:4], refs[4], refs[5]
    zh = lax.axis_index("replica") // 2 % 4
    near = zh + 1 - 2 * (zh % 2)
    count = take_count(parts, 256)
    for out, first in ((keep, zh), (send, near)):
        for i, block in enumerate((first, 3 - first)):
            cols = pl.ds(pl.multiple_of(block * 256, 256), 256)
            total = parts[0][0:256, cols].astype(F32)
            for p in parts[1:]:
                total = total + p[0:256, cols].astype(F32)
            out[0:256, 256 * i : 256 * i + 256] = total.astype(BF16)
        put_count(out, 256, count)


def halve_blocks(kept, recv, keep, send):
    count = take_count((kept, recv), 256)
    for i, out in enumerate((keep, send)):
        cols = slice(256 * i, 256 * i + 256)
        out[0:256, :] = (kept[0:256, cols].astype(F32) + recv[0:256, cols].astype(F32)).astype(BF16)
        put_count(out, 256, count)


def outer_step(*refs):
    parts, master, momentum, new_master, new_momentum = refs[:2], *refs[2:6]
    count = take_count(parts, 256)
    for c in (0, 128):
        cols = slice(c, c + 128)
        total = parts[0][0:256, cols].astype(F32) + parts[1][0:256, cols].astype(F32)
        pseudo_grad = master[:, cols] - total / count
        moved = momentum_decay * momentum[:, cols] + pseudo_grad
        new_momentum[:, cols] = moved
        new_master[:, cols] = master[:, cols] - outer_rate * (pseudo_grad + momentum_decay * moved)


def together(*groups):
    flat = lax.optimization_barrier(tuple(v for g in groups for v in g))
    out, i = [], 0
    for g in groups:
        out.append(list(flat[i : i + len(g)]))
        i += len(g)
    return out


def local(local_frag, master, momentum, counts, inputs, inner_weight, cotangent):
    dma = pltpu.SemaphoreType.DMA
    fsdp = lambda a, perm: lax.ppermute(a, "fsdp", perm)
    replica = lambda a, perm: lax.ppermute(a, "replica", perm)

    frag = local_frag[0]
    count = counts.astype(F32)
    frag_other, count_other = replica(frag, CORE_SWAP), replica(count, CORE_SWAP)

    sent = call(pack_weight, "pack_weight", [(HBM, inner_weight[0])], [(ANY, shape(ROWS, SEG))] * 4, [dma((4,))])
    got = {k: fsdp(sent[k], y_shift(k)) for k in (1, 3, 2)}
    got = [sent[0], got[1], got[2], got[3]]

    parts = call(
        weigh,
        "weigh",
        [(SMEM, count), (SMEM, count_other), (VMEM, frag), (VMEM, frag_other)],
        [(VMEM, shape(272, 1024))] * 4,
    )
    x1, x3 = replica(parts[1], x_shift(1)), replica(parts[3], x_shift(3))

    packed = call(
        pack_inputs,
        "pack_inputs",
        [(HBM, inputs), (HBM, cotangent)],
        [(ANY, shape(TOK + 32, SEG))] * 4,
        [dma((20,))],
    )
    packed, got = together(packed, got)
    (stacked,) = call(stack, "stack_weight", [(VMEM, a) for a in got], [(VMEM, shape(4 * ROWS, SEG))])
    crossed = fsdp(stacked, Z_SWAP)
    xs = [packed[0]] + [fsdp(packed[k], y_shift(k)) for k in (1, 2, 3)]
    got, (x1, x3, t2) = together(got, (x1, x3, parts[2]))
    parts = [parts[0], x1, replica(t2, x_shift(2)), x3]

    *back, w_full, cots = call(
        grad_to_inputs,
        "input_grad",
        [(VMEM, a) for a in (*got, crossed, *xs)],
        [(VMEM, shape(TOK, SEG))] * 4 + [(VMEM, shape(KVI, SEG)), (VMEM, shape(4 * TOK, KVI))],
    )
    back = [back[0]] + [fsdp(back[k], y_shift(-k)) for k in (1, 2, 3)]

    mine, other = call(
        functools.partial(weight_grad, 1.0 / (TOK * lax.axis_size("fsdp"))),
        "weight_grad",
        [(VMEM, a) for a in (*xs, cots)],
        [(VMEM, shape(4 * ROWS, SEG))] * 2,
        [pltpu.VMEM((KVI, SEG), BF16)],
    )
    recv = fsdp(other, Z_SWAP)
    (other,), parts = together((other,), parts)
    kept, send = call(sum_blocks, "sum_blocks", [(VMEM, a) for a in parts], [(VMEM, shape(272, 512))] * 2)
    near = replica(send, ZH_NEAR)
    keys = call(project, "project", [(VMEM, a) for a in (*xs, w_full)], [(VMEM, shape(TOK, KVI))] * 4)
    kept, send = call(
        halve_blocks, "halve_blocks", [(VMEM, kept), (VMEM, near)], [(VMEM, shape(272, 256))] * 2
    )
    far = replica(send, ZH_FAR)
    back, keys = together(back, keys)
    keys = [keys[0]] + [fsdp(keys[k], y_shift(-k)) for k in (1, 2, 3)]
    (back_full,) = call(
        unpack_columns, "unpack_input_grad", [(ANY, a) for a in back], [(ANY, shape(TOK, 8192))], [dma((4,))]
    )

    joined = call(
        join_grads,
        "join_grads",
        [(VMEM, mine), (VMEM, recv)],
        [(VMEM, shape(ROWS, SEG))] * 4,
    )
    joined = [joined[0]] + [fsdp(joined[j], y_shift(j)) for j in (1, 2, 3)]
    (projected,) = call(sum_keys, "sum_keys", [(VMEM, a) for a in keys], [(VMEM, shape(TOK, KVI))])
    new_master, new_momentum = call(
        outer_step,
        "outer_step",
        [(VMEM, a) for a in (kept, far, master, momentum)],
        [(VMEM, shape(256, 256, dtype=F32))] * 2,
    )
    (grads,) = call(finish, "finish", [(VMEM, a) for a in joined], [(VMEM, shape(ROWS, 8192))])
    return new_master, new_momentum, projected, back_full, grads[None]


def solution(mesh):
    placed = (
        P("replica", "fsdp", None),
        P("fsdp", "replica"),
        P("fsdp", "replica"),
        P("replica"),
        P(("replica", "fsdp"), None),
        P("replica", "fsdp", None),
        P(("replica", "fsdp"), None),
    )
    return jax.shard_map(
        local,
        mesh=mesh,
        in_specs=placed,
        out_specs=(
            P("fsdp", "replica"),
            P("fsdp", "replica"),
            P(("replica", "fsdp"), None),
            P(("replica", "fsdp"), None),
            P("replica", "fsdp", None),
        ),
        check_vma=False,
    )
```

```python
import functools

import jax
import jax.numpy as jnp
from jax import lax
from jax.experimental import pallas as pl
from jax.experimental.pallas import tpu as pltpu
from jax.sharding import PartitionSpec as P

momentum_decay = 0.9
outer_rate = 0.7

F32, BF16 = jnp.float32, jnp.bfloat16
ANY = pl.BlockSpec(memory_space=pl.ANY)
VMEM = pl.BlockSpec(memory_space=pltpu.VMEM)
SMEM = pl.BlockSpec(memory_space=pltpu.SMEM)
HBM = pl.BlockSpec(memory_space=pltpu.HBM)

SEG = 2048
ROWS = 64
TOK = 128
KVI = 512


def y_shift(k):
    return [(f, (f + 2 * k) % 8) for f in range(8)]


Z_SWAP = [(f, f ^ 1) for f in range(8)]
CORE_SWAP = [(r, r ^ 1) for r in range(32)]


X_NEAR = [(r, r ^ 8) for r in range(32)]
X_FAR = [(r, r ^ 24) for r in range(32)]
ZH_NEAR = [(r, r ^ 2) for r in range(32)]
ZH_FAR = [(r, r ^ 6) for r in range(32)]


def call(kernel, name, ins, outs, scratch=(), limit=24):
    arrays = [a for _, a in ins]
    return pl.pallas_call(
        kernel,
        name=name,
        in_specs=[s for s, _ in ins],
        out_specs=[s for s, _ in outs],
        out_shape=[o for _, o in outs],
        scratch_shapes=list(scratch),
        compiler_params=pltpu.CompilerParams(vmem_limit_bytes=limit << 20),
        cost_estimate=pl.CostEstimate(flops=0, bytes_accessed=0, transcendentals=0),
    )(*arrays)


def shape(*dims, dtype=BF16):
    return jax.ShapeDtypeStruct(dims, dtype)


def here():
    f = lax.axis_index("fsdp")
    return f // 2, f % 2


def run_all(copies):
    for c in copies:
        c.start()
    for c in copies:
        c.wait()


def pack_weight(w, *rest):
    outs, sems = rest[:4], rest[4]
    y, _ = here()
    copies = []
    for k in (1, 3, 2, 0):
        start = pl.multiple_of((y + k) % 4 * SEG, SEG)
        copies.append(pltpu.make_async_copy(w.at[:, pl.ds(start, SEG)], outs[k], sems.at[k]))
    run_all(copies)


def pack_inputs(x, cot, *rest):
    outs, sems = rest[:4], rest[4]
    y, _ = here()
    copies = []
    for k in range(4):
        start = pl.multiple_of((y + k) % 4 * SEG, SEG)
        copies.append((x.at[:, pl.ds(start, SEG)], outs[k].at[pl.ds(0, TOK)]))
        for j in range(4):
            copies.append((cot.at[pl.ds(32 * j, 32)], outs[k].at[pl.ds(TOK, 32), pl.ds(KVI * j, KVI)]))
    run_all([pltpu.make_async_copy(s, d, sems.at[i]) for i, (s, d) in enumerate(copies)])


def unpack_columns(*refs):
    parts, out, sems = refs[:4], refs[4], refs[5]
    y, _ = here()
    copies = []
    for k in range(4):
        start = pl.multiple_of((y + k) % 4 * SEG, SEG)
        copies.append(pltpu.make_async_copy(parts[k], out.at[:, pl.ds(start, SEG)], sems.at[k]))
    run_all(copies)


def stack(*refs):
    for k in range(4):
        refs[4][ROWS * k : ROWS * k + ROWS, :] = refs[k][0:ROWS, :]


def grad_to_inputs(*refs):
    got, other, xs, outs, w, turned, cots = refs[:4], refs[4], refs[5:9], refs[9:13], refs[13], refs[14], refs[15]
    y, z = here()
    for k in range(4):
        owner = (y + 4 - k) % 4
        w[pl.ds(pl.multiple_of((owner * 2 + z) * ROWS, ROWS), ROWS), :] = got[k][...]
        w[pl.ds(pl.multiple_of((owner * 2 + 1 - z) * ROWS, ROWS), ROWS), :] = other[ROWS * k : ROWS * k + ROWS, :]
        for j in range(4):
            cots[TOK * k + 32 * j : TOK * k + 32 * j + 32, :] = xs[k][TOK : TOK + 32, KVI * j : KVI * j + KVI]
    for c in range(0, SEG, 512):
        part = jnp.dot(cots[...], w[:, c : c + 512], preferred_element_type=F32).astype(BF16)
        for k in range(4):
            outs[k][:, c : c + 512] = part[TOK * k : TOK * k + TOK]
    turned[...] = cots[...].T


def weight_grad(scale, *refs):
    xs, turned, mine, other, whole = refs[:4], refs[4], refs[5], refs[6], refs[7]
    y, z = here()
    for c in range(0, SEG, 256):
        columns = jnp.concatenate([x[0:TOK, c : c + 256] for x in xs], axis=0)
        total = jnp.dot(turned[...], columns, preferred_element_type=F32)
        whole[:, c : c + 256] = (total * scale).astype(BF16)
    for j in range(4):
        to = (y + j) % 4 * 2
        rows = slice(ROWS * j, ROWS * j + ROWS)
        mine[rows, :] = whole[pl.ds(pl.multiple_of((to + z) * ROWS, ROWS), ROWS), :]
        other[rows, :] = whole[pl.ds(pl.multiple_of((to + 1 - z) * ROWS, ROWS), ROWS), :]


def project(*refs):
    xs, w, outs = refs[:4], refs[4], refs[5:9]
    total = None
    for c in range(0, SEG, 512):
        columns = jnp.concatenate([x[0:TOK, c : c + 512] for x in xs], axis=0)
        term = lax.dot_general(columns, w[:, c : c + 512], (((1,), (1,)), ((), ())), preferred_element_type=F32)
        total = term if total is None else total + term
    for k in range(4):
        outs[k][...] = total[TOK * k : TOK * k + TOK, :].astype(BF16)


def join_grads(mine, recv, *refs):
    parts, outs = refs[:4], refs[4:8]
    for j in range(4):
        rows = slice(ROWS * j, ROWS * j + ROWS)
        outs[j][0:ROWS, :] = (mine[rows, :].astype(F32) + recv[rows, :].astype(F32)).astype(BF16)
        for i in range(4):
            outs[j][ROWS : ROWS + 32, KVI * i : KVI * i + KVI] = parts[(4 - j) % 4][32 * i : 32 * i + 32, :]


def finish(*refs):
    got, grads, keys = refs[:4], refs[4], refs[5]
    y, _ = here()
    for j in range(4):
        owner = (y + 4 - j) % 4
        grads[:, pl.ds(pl.multiple_of(owner * SEG, SEG), SEG)] = got[j][0:ROWS, :]
    for i in range(4):
        total = None
        for j in range(4):
            term = got[j][ROWS : ROWS + 32, KVI * i : KVI * i + KVI].astype(F32)
            total = term if total is None else total + term
        keys[32 * i : 32 * i + 32, :] = total.astype(BF16)


def put_count(ref, row, value):
    half = ref.shape[1] // 2
    high = jnp.floor(value * (1.0 / 256.0))
    for i in range(0, half, 128):
        ref[row : row + 16, i : i + 128] = jnp.broadcast_to(high, (16, 128)).astype(BF16)
        ref[row : row + 16, half + i : half + i + 128] = jnp.broadcast_to(value - 256.0 * high, (16, 128)).astype(BF16)


def take_count(refs, row):
    half = refs[0].shape[1] // 2
    total = None
    for r in refs:
        high, low = r[row : row + 16, 0:128].astype(F32), r[row : row + 16, half : half + 128].astype(F32)
        term = high * 256.0 + low
        total = term if total is None else total + term
    return total[0:1, :]


def weigh(counts, counts_other, mine, other, keep, send):
    r = lax.axis_index("replica")
    x, core = r // 8, r % 2
    own, theirs = counts[0], counts_other[0]
    for out, first in ((keep, x), (send, x + 1 - 2 * (x % 2))):
        for i, block in enumerate((first, 3 - first)):
            for h in range(4):
                cols = pl.ds(pl.multiple_of(block * 2048 + h * 512 + core * 256, 256), 256)
                total = own * mine[:, cols].astype(F32) + theirs * other[:, cols].astype(F32)
                out[0:256, 1024 * i + 256 * h : 1024 * i + 256 * h + 256] = total.astype(BF16)
        put_count(out, 256, jnp.full((1, 128), own + theirs, F32))


def halve(kept, recv, keep, send):
    count = take_count((kept, recv), 256)
    width = kept.shape[1] // 2
    for i, out in enumerate((keep, send)):
        cols = slice(width * i, width * i + width)
        out[0:256, :] = (kept[0:256, cols].astype(F32) + recv[0:256, cols].astype(F32)).astype(BF16)
        put_count(out, 256, count)


def sum_blocks(kept, recv, keep, send):
    zh = lax.axis_index("replica") // 2 % 4
    count = take_count((kept, recv), 256)
    for out, first in ((keep, zh), (send, zh + 1 - 2 * (zh % 2))):
        for i, block in enumerate((first, 3 - first)):
            cols = pl.ds(pl.multiple_of(block * 256, 256), 256)
            total = kept[0:256, cols].astype(F32) + recv[0:256, cols].astype(F32)
            out[0:256, 256 * i : 256 * i + 256] = total.astype(BF16)
        put_count(out, 256, count)


def outer_step(*refs):
    parts, master, momentum, new_master, new_momentum = refs[:2], *refs[2:6]
    count = take_count(parts, 256)
    for c in (0, 128):
        cols = slice(c, c + 128)
        total = parts[0][0:256, cols].astype(F32) + parts[1][0:256, cols].astype(F32)
        pseudo_grad = master[:, cols] - total / count
        moved = momentum_decay * momentum[:, cols] + pseudo_grad
        new_momentum[:, cols] = moved
        new_master[:, cols] = master[:, cols] - outer_rate * (pseudo_grad + momentum_decay * moved)


def together(*groups):
    flat = lax.optimization_barrier(tuple(v for g in groups for v in g))
    out, i = [], 0
    for g in groups:
        out.append(list(flat[i : i + len(g)]))
        i += len(g)
    return out


def local(local_frag, master, momentum, counts, inputs, inner_weight, cotangent):
    dma = pltpu.SemaphoreType.DMA
    fsdp = lambda a, perm: lax.ppermute(a, "fsdp", perm)
    replica = lambda a, perm: lax.ppermute(a, "replica", perm)

    frag = local_frag[0]
    count = counts.astype(F32)
    frag_other, count_other = replica(frag, CORE_SWAP), replica(count, CORE_SWAP)

    sent = call(pack_weight, "pack_weight", [(HBM, inner_weight[0])], [(ANY, shape(ROWS, SEG))] * 4, [dma((4,))])
    got = {k: fsdp(sent[k], y_shift(k)) for k in (1, 3, 2)}
    got = [sent[0], got[1], got[2], got[3]]

    kept, send = call(
        weigh,
        "weigh",
        [(SMEM, count), (SMEM, count_other), (VMEM, frag), (VMEM, frag_other)],
        [(VMEM, shape(272, 2048))] * 2,
    )
    x_near = replica(send, X_NEAR)

    packed = call(
        pack_inputs,
        "pack_inputs",
        [(HBM, inputs), (HBM, cotangent)],
        [(ANY, shape(TOK + 32, SEG))] * 4,
        [dma((20,))],
    )
    packed, got = together(packed, got)
    (stacked,) = call(stack, "stack_weight", [(VMEM, a) for a in got], [(VMEM, shape(4 * ROWS, SEG))])
    crossed = fsdp(stacked, Z_SWAP)
    xs = [packed[0]] + [fsdp(packed[k], y_shift(k)) for k in (1, 2, 3)]
    kept, send = call(halve, "halve_x", [(VMEM, kept), (VMEM, x_near)], [(VMEM, shape(272, 1024))] * 2)
    got, (kept, send) = together(got, (kept, send))
    x_far = replica(send, X_FAR)

    *back, w_full, turned = call(
        grad_to_inputs,
        "input_grad",
        [(VMEM, a) for a in (*got, crossed, *xs)],
        [(VMEM, shape(TOK, SEG))] * 4 + [(VMEM, shape(KVI, SEG)), (VMEM, shape(KVI, 4 * TOK))],
        [pltpu.VMEM((4 * TOK, KVI), BF16)],
    )
    mine, other = call(
        functools.partial(weight_grad, 1.0 / (TOK * lax.axis_size("fsdp"))),
        "weight_grad",
        [(VMEM, a) for a in (*xs, turned)],
        [(VMEM, shape(4 * ROWS, SEG))] * 2,
        [pltpu.VMEM((KVI, SEG), BF16)],
    )
    back = [back[0]] + [fsdp(back[k], y_shift(-k)) for k in (1, 2, 3)]
    recv = fsdp(other, Z_SWAP)
    kept, send = call(sum_blocks, "sum_blocks", [(VMEM, kept), (VMEM, x_far)], [(VMEM, shape(272, 512))] * 2)
    (send,), (w_full,) = together((send,), (w_full,))
    near = replica(send, ZH_NEAR)
    keys = call(project, "project", [(VMEM, a) for a in (*xs, w_full)], [(VMEM, shape(TOK, KVI))] * 4)
    (recv,), back = together((recv,), back)
    joined = call(
        join_grads,
        "join_grads",
        [(VMEM, a) for a in (mine, recv, *keys)],
        [(VMEM, shape(ROWS + 32, SEG))] * 4,
    )
    joined = [joined[0]] + [fsdp(joined[j], y_shift(j)) for j in (1, 2, 3)]
    (back_full,) = call(
        unpack_columns, "unpack_input_grad", [(ANY, a) for a in back], [(ANY, shape(TOK, 8192))], [dma((4,))]
    )
    kept, send = call(halve, "halve_z", [(VMEM, kept), (VMEM, near)], [(VMEM, shape(272, 256))] * 2)
    far = replica(send, ZH_FAR)
    new_master, new_momentum = call(
        outer_step,
        "outer_step",
        [(VMEM, a) for a in (kept, far, master, momentum)],
        [(VMEM, shape(256, 256, dtype=F32))] * 2,
    )
    grads, projected = call(
        finish, "finish", [(VMEM, a) for a in joined], [(VMEM, shape(ROWS, 8192)), (VMEM, shape(TOK, KVI))]
    )
    return new_master, new_momentum, projected, back_full, grads[None]


def solution(mesh):
    placed = (
        P("replica", "fsdp", None),
        P("fsdp", "replica"),
        P("fsdp", "replica"),
        P("replica"),
        P(("replica", "fsdp"), None),
        P("replica", "fsdp", None),
        P(("replica", "fsdp"), None),
    )
    return jax.shard_map(
        local,
        mesh=mesh,
        in_specs=placed,
        out_specs=(
            P("fsdp", "replica"),
            P("fsdp", "replica"),
            P(("replica", "fsdp"), None),
            P(("replica", "fsdp"), None),
            P("replica", "fsdp", None),
        ),
        check_vma=False,
    )
```

```python
import functools

import jax
import jax.numpy as jnp
from jax import lax
from jax.experimental import pallas as pl
from jax.experimental.pallas import tpu as pltpu
from jax.sharding import PartitionSpec as P

momentum_decay = 0.9
outer_rate = 0.7

F32, BF16 = jnp.float32, jnp.bfloat16
ANY = pl.BlockSpec(memory_space=pl.ANY)
VMEM = pl.BlockSpec(memory_space=pltpu.VMEM)
SMEM = pl.BlockSpec(memory_space=pltpu.SMEM)
HBM = pl.BlockSpec(memory_space=pltpu.HBM)

SEG = 2048
ROWS = 64
TOK = 128
KVI = 512


def y_shift(k):
    return [(f, (f + 2 * k) % 8) for f in range(8)]


Z_SWAP = [(f, f ^ 1) for f in range(8)]
CORE_SWAP = [(r, r ^ 1) for r in range(32)]


X_NEAR = [(r, r ^ 8) for r in range(32)]
X_FAR = [(r, r ^ 24) for r in range(32)]
ZH_NEAR = [(r, r ^ 2) for r in range(32)]
ZH_FAR = [(r, r ^ 6) for r in range(32)]


def call(kernel, name, ins, outs, scratch=(), limit=24):
    arrays = [a for _, a in ins]
    return pl.pallas_call(
        kernel,
        name=name,
        in_specs=[s for s, _ in ins],
        out_specs=[s for s, _ in outs],
        out_shape=[o for _, o in outs],
        scratch_shapes=list(scratch),
        compiler_params=pltpu.CompilerParams(vmem_limit_bytes=limit << 20),
        cost_estimate=pl.CostEstimate(flops=0, bytes_accessed=0, transcendentals=0),
    )(*arrays)


def shape(*dims, dtype=BF16):
    return jax.ShapeDtypeStruct(dims, dtype)


def here():
    f = lax.axis_index("fsdp")
    return f // 2, f % 2


def run_all(copies):
    for c in copies:
        c.start()
    for c in copies:
        c.wait()


def pack_weight(w, cot, *rest):
    outs, sems = rest[:4], rest[4]
    y, _ = here()
    copies = []
    for k in (2, 1, 3, 0):
        start = pl.multiple_of((y + k) % 4 * SEG, SEG)
        copies.append((w.at[:, pl.ds(start, SEG)], outs[k].at[pl.ds(0, ROWS)]))
        for j in range(4):
            copies.append((cot.at[pl.ds(32 * j, 32)], outs[k].at[pl.ds(ROWS, 32), pl.ds(KVI * j, KVI)]))
    run_all([pltpu.make_async_copy(s, d, sems.at[i]) for i, (s, d) in enumerate(copies)])


def pack_inputs(x, *rest):
    outs, sems = rest[:4], rest[4]
    y, _ = here()
    copies = []
    for k in range(4):
        start = pl.multiple_of((y + k) % 4 * SEG, SEG)
        copies.append(pltpu.make_async_copy(x.at[:, pl.ds(start, SEG)], outs[k], sems.at[k]))
    run_all(copies)


def unpack_columns(*refs):
    parts, out, sems = refs[:4], refs[4], refs[5]
    y, _ = here()
    copies = []
    for k in range(4):
        start = pl.multiple_of((y + k) % 4 * SEG, SEG)
        copies.append(pltpu.make_async_copy(parts[k], out.at[:, pl.ds(start, SEG)], sems.at[k]))
    run_all(copies)


def stack(*refs):
    for k in range(4):
        refs[4][ROWS * k : ROWS * k + ROWS, :] = refs[k][0:ROWS, :]


def grad_to_inputs(*refs):
    got, other, outs, w, turned, cots = refs[:4], refs[4], refs[5:9], refs[9], refs[10], refs[11]
    y, z = here()
    for k in range(4):
        owner = (y + 4 - k) % 4
        w[pl.ds(pl.multiple_of((owner * 2 + z) * ROWS, ROWS), ROWS), :] = got[k][0:ROWS, :]
        w[pl.ds(pl.multiple_of((owner * 2 + 1 - z) * ROWS, ROWS), ROWS), :] = other[ROWS * k : ROWS * k + ROWS, :]
        for j in range(4):
            cots[TOK * k + 32 * j : TOK * k + 32 * j + 32, :] = got[k][ROWS : ROWS + 32, KVI * j : KVI * j + KVI]
    for c in range(0, SEG, 512):
        part = jnp.dot(cots[...], w[:, c : c + 512], preferred_element_type=F32).astype(BF16)
        for k in range(4):
            outs[k][:, c : c + 512] = part[TOK * k : TOK * k + TOK]
    turned[...] = cots[...].T


def weight_grad(scale, *refs):
    xs, turned, mine, other, whole = refs[:4], refs[4], refs[5], refs[6], refs[7]
    y, z = here()
    for c in range(0, SEG, 256):
        columns = jnp.concatenate([x[:, c : c + 256] for x in xs], axis=0)
        total = jnp.dot(turned[...], columns, preferred_element_type=F32)
        whole[:, c : c + 256] = (total * scale).astype(BF16)
    for j in range(4):
        to = (y + j) % 4 * 2
        rows = slice(ROWS * j, ROWS * j + ROWS)
        mine[rows, :] = whole[pl.ds(pl.multiple_of((to + z) * ROWS, ROWS), ROWS), :]
        other[rows, :] = whole[pl.ds(pl.multiple_of((to + 1 - z) * ROWS, ROWS), ROWS), :]


def project(*refs):
    xs, w, outs = refs[:4], refs[4], refs[5:9]
    total = None
    for c in range(0, SEG, 512):
        columns = jnp.concatenate([x[:, c : c + 512] for x in xs], axis=0)
        term = lax.dot_general(columns, w[:, c : c + 512], (((1,), (1,)), ((), ())), preferred_element_type=F32)
        total = term if total is None else total + term
    for k in range(4):
        outs[k][...] = total[TOK * k : TOK * k + TOK, :].astype(BF16)


def join_grads(mine, recv, *refs):
    parts, outs = refs[:4], refs[4:8]
    for j in range(4):
        rows = slice(ROWS * j, ROWS * j + ROWS)
        outs[j][0:ROWS, :] = (mine[rows, :].astype(F32) + recv[rows, :].astype(F32)).astype(BF16)
        for i in range(4):
            outs[j][ROWS : ROWS + 32, KVI * i : KVI * i + KVI] = parts[(4 - j) % 4][32 * i : 32 * i + 32, :]


def finish(*refs):
    got, grads, keys = refs[:4], refs[4], refs[5]
    y, _ = here()
    for j in range(4):
        owner = (y + 4 - j) % 4
        grads[:, pl.ds(pl.multiple_of(owner * SEG, SEG), SEG)] = got[j][0:ROWS, :]
    for i in range(4):
        total = None
        for j in range(4):
            term = got[j][ROWS : ROWS + 32, KVI * i : KVI * i + KVI].astype(F32)
            total = term if total is None else total + term
        keys[32 * i : 32 * i + 32, :] = total.astype(BF16)


def put_count(ref, row, value):
    half = ref.shape[1] // 2
    high = jnp.floor(value * (1.0 / 256.0))
    for i in range(0, half, 128):
        ref[row : row + 16, i : i + 128] = jnp.broadcast_to(high, (16, 128)).astype(BF16)
        ref[row : row + 16, half + i : half + i + 128] = jnp.broadcast_to(value - 256.0 * high, (16, 128)).astype(BF16)


def take_count(refs, row):
    half = refs[0].shape[1] // 2
    total = None
    for r in refs:
        high, low = r[row : row + 16, 0:128].astype(F32), r[row : row + 16, half : half + 128].astype(F32)
        term = high * 256.0 + low
        total = term if total is None else total + term
    return total[0:1, :]


def weigh(counts, counts_other, mine, other, keep, send):
    r = lax.axis_index("replica")
    x, core = r // 8, r % 2
    own, theirs = counts[0], counts_other[0]
    for out, first in ((keep, x), (send, x + 1 - 2 * (x % 2))):
        for i, block in enumerate((first, 3 - first)):
            for h in range(4):
                cols = pl.ds(pl.multiple_of(block * 2048 + h * 512 + core * 256, 256), 256)
                total = own * mine[:, cols].astype(F32) + theirs * other[:, cols].astype(F32)
                out[0:256, 1024 * i + 256 * h : 1024 * i + 256 * h + 256] = total.astype(BF16)
        put_count(out, 256, jnp.full((1, 128), own + theirs, F32))


def halve(kept, recv, keep, send):
    count = take_count((kept, recv), 256)
    width = kept.shape[1] // 2
    for i, out in enumerate((keep, send)):
        cols = slice(width * i, width * i + width)
        out[0:256, :] = (kept[0:256, cols].astype(F32) + recv[0:256, cols].astype(F32)).astype(BF16)
        put_count(out, 256, count)


def sum_blocks(kept, recv, keep, send):
    zh = lax.axis_index("replica") // 2 % 4
    count = take_count((kept, recv), 256)
    for out, first in ((keep, zh), (send, zh + 1 - 2 * (zh % 2))):
        for i, block in enumerate((first, 3 - first)):
            cols = pl.ds(pl.multiple_of(block * 256, 256), 256)
            total = kept[0:256, cols].astype(F32) + recv[0:256, cols].astype(F32)
            out[0:256, 256 * i : 256 * i + 256] = total.astype(BF16)
        put_count(out, 256, count)


def outer_step(*refs):
    parts, master, momentum, new_master, new_momentum = refs[:2], *refs[2:6]
    count = take_count(parts, 256)
    for c in (0, 128):
        cols = slice(c, c + 128)
        total = parts[0][0:256, cols].astype(F32) + parts[1][0:256, cols].astype(F32)
        pseudo_grad = master[:, cols] - total / count
        moved = momentum_decay * momentum[:, cols] + pseudo_grad
        new_momentum[:, cols] = moved
        new_master[:, cols] = master[:, cols] - outer_rate * (pseudo_grad + momentum_decay * moved)


def together(*groups):
    flat = lax.optimization_barrier(tuple(v for g in groups for v in g))
    out, i = [], 0
    for g in groups:
        out.append(list(flat[i : i + len(g)]))
        i += len(g)
    return out


def local(local_frag, master, momentum, counts, inputs, inner_weight, cotangent):
    dma = pltpu.SemaphoreType.DMA
    fsdp = lambda a, perm: lax.ppermute(a, "fsdp", perm)
    replica = lambda a, perm: lax.ppermute(a, "replica", perm)

    frag = local_frag[0]
    count = counts.astype(F32)
    frag_other, count_other = replica(frag, CORE_SWAP), replica(count, CORE_SWAP)

    sent = call(
        pack_weight,
        "pack_weight",
        [(HBM, inner_weight[0]), (HBM, cotangent)],
        [(ANY, shape(ROWS + 32, SEG))] * 4,
        [dma((20,))],
    )
    got = {k: fsdp(sent[k], y_shift(k)) for k in (1, 3, 2)}
    got = [sent[0], got[1], got[2], got[3]]

    kept, send = call(
        weigh,
        "weigh",
        [(SMEM, count), (SMEM, count_other), (VMEM, frag), (VMEM, frag_other)],
        [(VMEM, shape(272, 2048))] * 2,
    )
    x_near = replica(send, X_NEAR)

    packed = call(pack_inputs, "pack_inputs", [(HBM, inputs)], [(ANY, shape(TOK, SEG))] * 4, [dma((4,))])
    packed, got = together(packed, got)
    (stacked,) = call(stack, "stack_weight", [(VMEM, a) for a in got], [(VMEM, shape(4 * ROWS, SEG))])
    crossed = fsdp(stacked, Z_SWAP)
    xs = [packed[0]] + [fsdp(packed[k], y_shift(k)) for k in (1, 2, 3)]
    kept, send = call(halve, "halve_x", [(VMEM, kept), (VMEM, x_near)], [(VMEM, shape(272, 1024))] * 2)
    got, (kept, send) = together(got, (kept, send))
    x_far = replica(send, X_FAR)

    *back, w_full, turned = call(
        grad_to_inputs,
        "input_grad",
        [(VMEM, a) for a in (*got, crossed)],
        [(VMEM, shape(TOK, SEG))] * 4 + [(VMEM, shape(KVI, SEG)), (VMEM, shape(KVI, 4 * TOK))],
        [pltpu.VMEM((4 * TOK, KVI), BF16)],
    )
    mine, other = call(
        functools.partial(weight_grad, 1.0 / (TOK * lax.axis_size("fsdp"))),
        "weight_grad",
        [(VMEM, a) for a in (*xs, turned)],
        [(VMEM, shape(4 * ROWS, SEG))] * 2,
        [pltpu.VMEM((KVI, SEG), BF16)],
    )
    back, (x_far,) = together(back, (x_far,))
    back = [back[0]] + [fsdp(back[k], y_shift(-k)) for k in (1, 2, 3)]
    recv = fsdp(other, Z_SWAP)
    kept, send = call(sum_blocks, "sum_blocks", [(VMEM, kept), (VMEM, x_far)], [(VMEM, shape(272, 512))] * 2)
    (send,), (w_full,) = together((send,), (w_full,))
    near = replica(send, ZH_NEAR)
    keys = call(project, "project", [(VMEM, a) for a in (*xs, w_full)], [(VMEM, shape(TOK, KVI))] * 4)
    (recv,), back = together((recv,), back)
    joined = call(
        join_grads,
        "join_grads",
        [(VMEM, a) for a in (mine, recv, *keys)],
        [(VMEM, shape(ROWS + 32, SEG))] * 4,
    )
    joined = [joined[0]] + [fsdp(joined[j], y_shift(j)) for j in (1, 2, 3)]
    (back_full,) = call(
        unpack_columns, "unpack_input_grad", [(ANY, a) for a in back], [(ANY, shape(TOK, 8192))], [dma((4,))]
    )
    kept, send = call(halve, "halve_z", [(VMEM, kept), (VMEM, near)], [(VMEM, shape(272, 256))] * 2)
    far = replica(send, ZH_FAR)
    new_master, new_momentum = call(
        outer_step,
        "outer_step",
        [(VMEM, a) for a in (kept, far, master, momentum)],
        [(VMEM, shape(256, 256, dtype=F32))] * 2,
    )
    grads, projected = call(
        finish, "finish", [(VMEM, a) for a in joined], [(VMEM, shape(ROWS, 8192)), (VMEM, shape(TOK, KVI))]
    )
    return new_master, new_momentum, projected, back_full, grads[None]


def solution(mesh):
    placed = (
        P("replica", "fsdp", None),
        P("fsdp", "replica"),
        P("fsdp", "replica"),
        P("replica"),
        P(("replica", "fsdp"), None),
        P("replica", "fsdp", None),
        P(("replica", "fsdp"), None),
    )
    return jax.shard_map(
        local,
        mesh=mesh,
        in_specs=placed,
        out_specs=(
            P("fsdp", "replica"),
            P("fsdp", "replica"),
            P(("replica", "fsdp"), None),
            P(("replica", "fsdp"), None),
            P("replica", "fsdp", None),
        ),
        check_vma=False,
    )
```

```python
import functools

import jax
import jax.numpy as jnp
from jax import lax
from jax.experimental import pallas as pl
from jax.experimental.pallas import tpu as pltpu
from jax.sharding import PartitionSpec as P

momentum_decay = 0.9
outer_rate = 0.7

F32, BF16 = jnp.float32, jnp.bfloat16
ANY = pl.BlockSpec(memory_space=pl.ANY)
VMEM = pl.BlockSpec(memory_space=pltpu.VMEM)
SMEM = pl.BlockSpec(memory_space=pltpu.SMEM)
HBM = pl.BlockSpec(memory_space=pltpu.HBM)

SEG = 2048
ROWS = 64
TOK = 128
KVI = 512


def y_shift(k):
    return [(f, (f + 2 * k) % 8) for f in range(8)]


Z_SWAP = [(f, f ^ 1) for f in range(8)]
CORE_SWAP = [(r, r ^ 1) for r in range(32)]


X_NEAR = [(r, r ^ 8) for r in range(32)]
X_FAR = [(r, r ^ 24) for r in range(32)]
ZH_NEAR = [(r, r ^ 2) for r in range(32)]
ZH_FAR = [(r, r ^ 6) for r in range(32)]


def call(kernel, name, ins, outs, scratch=(), limit=24):
    arrays = [a for _, a in ins]
    return pl.pallas_call(
        kernel,
        name=name,
        in_specs=[s for s, _ in ins],
        out_specs=[s for s, _ in outs],
        out_shape=[o for _, o in outs],
        scratch_shapes=list(scratch),
        compiler_params=pltpu.CompilerParams(vmem_limit_bytes=limit << 20),
        cost_estimate=pl.CostEstimate(flops=0, bytes_accessed=0, transcendentals=0),
    )(*arrays)


def shape(*dims, dtype=BF16):
    return jax.ShapeDtypeStruct(dims, dtype)


def here():
    f = lax.axis_index("fsdp")
    return f // 2, f % 2


def run_all(copies):
    for c in copies:
        c.start()
    for c in copies:
        c.wait()


def pack_weight(w, cot, *rest):
    outs, sems = rest[:4], rest[4]
    y, _ = here()
    copies = []
    for k in (2, 1, 3, 0):
        start = pl.multiple_of((y + k) % 4 * SEG, SEG)
        copies.append((w.at[:, pl.ds(start, SEG)], outs[k].at[pl.ds(0, ROWS)]))
        for j in range(4):
            copies.append((cot.at[pl.ds(32 * j, 32)], outs[k].at[pl.ds(ROWS, 32), pl.ds(KVI * j, KVI)]))
    run_all([pltpu.make_async_copy(s, d, sems.at[i]) for i, (s, d) in enumerate(copies)])


def pack_inputs(x, *rest):
    outs, sems = rest[:4], rest[4]
    y, _ = here()
    copies = []
    for k in range(4):
        start = pl.multiple_of((y + k) % 4 * SEG, SEG)
        copies.append(pltpu.make_async_copy(x.at[:, pl.ds(start, SEG)], outs[k], sems.at[k]))
    run_all(copies)


def unpack_columns(*refs):
    parts, out, sems = refs[:4], refs[4], refs[5]
    y, _ = here()
    copies = []
    for k in range(4):
        start = pl.multiple_of((y + k) % 4 * SEG, SEG)
        copies.append(pltpu.make_async_copy(parts[k], out.at[:, pl.ds(start, SEG)], sems.at[k]))
    run_all(copies)


def stack(*refs):
    for k in range(4):
        refs[4][ROWS * k : ROWS * k + ROWS, :] = refs[k][0:ROWS, :]


def grad_to_inputs(*refs):
    got, other, outs, w, turned, cots = refs[:4], refs[4], refs[5:9], refs[9], refs[10], refs[11]
    y, z = here()
    for k in range(4):
        owner = (y + 4 - k) % 4
        w[pl.ds(pl.multiple_of((owner * 2 + z) * ROWS, ROWS), ROWS), :] = got[k][0:ROWS, :]
        w[pl.ds(pl.multiple_of((owner * 2 + 1 - z) * ROWS, ROWS), ROWS), :] = other[ROWS * k : ROWS * k + ROWS, :]
        for j in range(4):
            cots[TOK * k + 32 * j : TOK * k + 32 * j + 32, :] = got[k][ROWS : ROWS + 32, KVI * j : KVI * j + KVI]
    for c in range(0, SEG, 512):
        part = jnp.dot(cots[...], w[:, c : c + 512], preferred_element_type=F32).astype(BF16)
        for k in range(4):
            outs[k][:, c : c + 512] = part[TOK * k : TOK * k + TOK]
    turned[...] = cots[...].T


def weight_grad(scale, *refs):
    xs, turned, mine, other, whole = refs[:4], refs[4], refs[5], refs[6], refs[7]
    y, z = here()
    for c in range(0, SEG, 256):
        columns = jnp.concatenate([x[:, c : c + 256] for x in xs], axis=0)
        total = jnp.dot(turned[...], columns, preferred_element_type=F32)
        whole[:, c : c + 256] = (total * scale).astype(BF16)
    for j in range(4):
        to = (y + j) % 4 * 2
        rows = slice(ROWS * j, ROWS * j + ROWS)
        mine[rows, :] = whole[pl.ds(pl.multiple_of((to + z) * ROWS, ROWS), ROWS), :]
        other[rows, :] = whole[pl.ds(pl.multiple_of((to + 1 - z) * ROWS, ROWS), ROWS), :]


def project(*refs):
    xs, w, outs = refs[:4], refs[4], refs[5:9]
    total = None
    for c in range(0, SEG, 512):
        columns = jnp.concatenate([x[:, c : c + 512] for x in xs], axis=0)
        term = lax.dot_general(columns, w[:, c : c + 512], (((1,), (1,)), ((), ())), preferred_element_type=F32)
        total = term if total is None else total + term
    for k in range(4):
        outs[k][...] = total[TOK * k : TOK * k + TOK, :].astype(BF16)


def join_grads(mine, recv, *refs):
    parts, outs = refs[:4], refs[4:8]
    for j in range(4):
        rows = slice(ROWS * j, ROWS * j + ROWS)
        outs[j][0:ROWS, :] = (mine[rows, :].astype(F32) + recv[rows, :].astype(F32)).astype(BF16)
        for i in range(4):
            outs[j][ROWS : ROWS + 32, KVI * i : KVI * i + KVI] = parts[(4 - j) % 4][32 * i : 32 * i + 32, :]


def finish(*refs):
    got, grads, keys = refs[:4], refs[4], refs[5]
    y, _ = here()
    for j in range(4):
        owner = (y + 4 - j) % 4
        grads[:, pl.ds(pl.multiple_of(owner * SEG, SEG), SEG)] = got[j][0:ROWS, :]
    for i in range(4):
        total = None
        for j in range(4):
            term = got[j][ROWS : ROWS + 32, KVI * i : KVI * i + KVI].astype(F32)
            total = term if total is None else total + term
        keys[32 * i : 32 * i + 32, :] = total.astype(BF16)


def put_count(ref, row, value):
    half = ref.shape[1] // 2
    high = jnp.floor(value * (1.0 / 256.0))
    for i in range(0, half, 128):
        ref[row : row + 16, i : i + 128] = jnp.broadcast_to(high, (16, 128)).astype(BF16)
        ref[row : row + 16, half + i : half + i + 128] = jnp.broadcast_to(value - 256.0 * high, (16, 128)).astype(BF16)


def take_count(refs, row):
    half = refs[0].shape[1] // 2
    total = None
    for r in refs:
        high, low = r[row : row + 16, 0:128].astype(F32), r[row : row + 16, half : half + 128].astype(F32)
        term = high * 256.0 + low
        total = term if total is None else total + term
    return total[0:1, :]


def weigh(counts, counts_other, mine, other, keep, send):
    r = lax.axis_index("replica")
    x, core = r // 8, r % 2
    own, theirs = counts[0], counts_other[0]
    for out, first in ((keep, x), (send, x + 1 - 2 * (x % 2))):
        for i, block in enumerate((first, 3 - first)):
            for h in range(4):
                cols = pl.ds(pl.multiple_of(block * 2048 + h * 512 + core * 256, 256), 256)
                total = own * mine[:, cols].astype(F32) + theirs * other[:, cols].astype(F32)
                out[0:256, 1024 * i + 256 * h : 1024 * i + 256 * h + 256] = total.astype(BF16)
        put_count(out, 256, jnp.full((1, 128), own + theirs, F32))


def halve(kept, recv, keep, send):
    count = take_count((kept, recv), 256)
    width = kept.shape[1] // 2
    for i, out in enumerate((keep, send)):
        cols = slice(width * i, width * i + width)
        out[0:256, :] = (kept[0:256, cols].astype(F32) + recv[0:256, cols].astype(F32)).astype(BF16)
        put_count(out, 256, count)


def sum_blocks(kept, recv, keep, send):
    zh = lax.axis_index("replica") // 2 % 4
    count = take_count((kept, recv), 256)
    for out, first in ((keep, zh), (send, zh + 1 - 2 * (zh % 2))):
        for i, block in enumerate((first, 3 - first)):
            cols = pl.ds(pl.multiple_of(block * 256, 256), 256)
            total = kept[0:256, cols].astype(F32) + recv[0:256, cols].astype(F32)
            out[0:256, 256 * i : 256 * i + 256] = total.astype(BF16)
        put_count(out, 256, count)


def outer_step(*refs):
    parts, master, momentum, new_master, new_momentum = refs[:2], *refs[2:6]
    count = take_count(parts, 256)
    for c in (0, 128):
        cols = slice(c, c + 128)
        total = parts[0][0:256, cols].astype(F32) + parts[1][0:256, cols].astype(F32)
        pseudo_grad = master[:, cols] - total / count
        moved = momentum_decay * momentum[:, cols] + pseudo_grad
        new_momentum[:, cols] = moved
        new_master[:, cols] = master[:, cols] - outer_rate * (pseudo_grad + momentum_decay * moved)


def together(*groups):
    flat = lax.optimization_barrier(tuple(v for g in groups for v in g))
    out, i = [], 0
    for g in groups:
        out.append(list(flat[i : i + len(g)]))
        i += len(g)
    return out


def local(local_frag, master, momentum, counts, inputs, inner_weight, cotangent):
    dma = pltpu.SemaphoreType.DMA
    fsdp = lambda a, perm: lax.ppermute(a, "fsdp", perm)
    replica = lambda a, perm: lax.ppermute(a, "replica", perm)

    frag = local_frag[0]
    count = counts.astype(F32)
    frag_other, count_other = replica(frag, CORE_SWAP), replica(count, CORE_SWAP)

    sent = call(
        pack_weight,
        "pack_weight",
        [(HBM, inner_weight[0]), (HBM, cotangent)],
        [(ANY, shape(ROWS + 32, SEG))] * 4,
        [dma((20,))],
    )
    got = {k: fsdp(sent[k], y_shift(k)) for k in (1, 3, 2)}
    got = [sent[0], got[1], got[2], got[3]]

    kept, send = call(
        weigh,
        "weigh",
        [(SMEM, count), (SMEM, count_other), (VMEM, frag), (VMEM, frag_other)],
        [(VMEM, shape(272, 2048))] * 2,
    )
    x_near = replica(send, X_NEAR)

    packed = call(pack_inputs, "pack_inputs", [(HBM, inputs)], [(ANY, shape(TOK, SEG))] * 4, [dma((4,))])
    packed, got = together(packed, got)
    (stacked,) = call(stack, "stack_weight", [(VMEM, a) for a in got], [(VMEM, shape(4 * ROWS, SEG))])
    crossed = fsdp(stacked, Z_SWAP)
    xs = [packed[0]] + [fsdp(packed[k], y_shift(k)) for k in (1, 2, 3)]
    kept, send = call(halve, "halve_x", [(VMEM, kept), (VMEM, x_near)], [(VMEM, shape(272, 1024))] * 2)
    got, (kept, send) = together(got, (kept, send))
    x_far = replica(send, X_FAR)

    *back, w_full, turned = call(
        grad_to_inputs,
        "input_grad",
        [(VMEM, a) for a in (*got, crossed)],
        [(VMEM, shape(TOK, SEG))] * 4 + [(VMEM, shape(KVI, SEG)), (VMEM, shape(KVI, 4 * TOK))],
        [pltpu.VMEM((4 * TOK, KVI), BF16)],
    )
    mine, other = call(
        functools.partial(weight_grad, 1.0 / (TOK * lax.axis_size("fsdp"))),
        "weight_grad",
        [(VMEM, a) for a in (*xs, turned)],
        [(VMEM, shape(4 * ROWS, SEG))] * 2,
        [pltpu.VMEM((KVI, SEG), BF16)],
    )
    back, (x_far,) = together(back, (x_far,))
    back = [back[0]] + [fsdp(back[k], y_shift(-k)) for k in (1, 2, 3)]
    recv = fsdp(other, Z_SWAP)
    kept, send = call(sum_blocks, "sum_blocks", [(VMEM, kept), (VMEM, x_far)], [(VMEM, shape(272, 512))] * 2)
    (send,), (w_full,) = together((send,), (w_full,))
    keys = call(project, "project", [(VMEM, a) for a in (*xs, w_full)], [(VMEM, shape(TOK, KVI))] * 4)
    (recv,), (back[1], back[2]) = together((recv,), (back[1], back[2]))
    joined = call(
        join_grads,
        "join_grads",
        [(VMEM, a) for a in (mine, recv, *keys)],
        [(VMEM, shape(ROWS + 32, SEG))] * 4,
    )
    joined, (send,) = together(joined, (send,))
    near = replica(send, ZH_NEAR)
    joined = [joined[0]] + [fsdp(joined[j], y_shift(j)) for j in (1, 2, 3)]
    (back_full,) = call(
        unpack_columns, "unpack_input_grad", [(ANY, a) for a in back], [(ANY, shape(TOK, 8192))], [dma((4,))]
    )
    kept, send = call(halve, "halve_z", [(VMEM, kept), (VMEM, near)], [(VMEM, shape(272, 256))] * 2)
    far = replica(send, ZH_FAR)
    new_master, new_momentum = call(
        outer_step,
        "outer_step",
        [(VMEM, a) for a in (kept, far, master, momentum)],
        [(VMEM, shape(256, 256, dtype=F32))] * 2,
    )
    joined, (new_master, new_momentum) = together(joined, (new_master, new_momentum))
    grads, projected = call(
        finish, "finish", [(VMEM, a) for a in joined], [(VMEM, shape(ROWS, 8192)), (VMEM, shape(TOK, KVI))]
    )
    return new_master, new_momentum, projected, back_full, grads[None]


def solution(mesh):
    placed = (
        P("replica", "fsdp", None),
        P("fsdp", "replica"),
        P("fsdp", "replica"),
        P("replica"),
        P(("replica", "fsdp"), None),
        P("replica", "fsdp", None),
        P(("replica", "fsdp"), None),
    )
    return jax.shard_map(
        local,
        mesh=mesh,
        in_specs=placed,
        out_specs=(
            P("fsdp", "replica"),
            P("fsdp", "replica"),
            P(("replica", "fsdp"), None),
            P(("replica", "fsdp"), None),
            P("replica", "fsdp", None),
        ),
        check_vma=False,
    )
```
